32 devices in a mesh: dp: 16 (over z, y, core), rep: 2 (over x).
Axes of the slice: x: 2, y: 2, z: 4, core: 2. Of those that a mesh axis runs over, the one named last changes fastest.
Arguments:
- picture_vectors: bfloat16 [8192, 1152], P('dp'), may hold values from -1 to 1
- caption_vectors: bfloat16 [8192, 1152], P('dp'), may hold values from -1 to 1
- matched_caption_index: int32 [16, 512], P('dp'), may hold values from 0 to 511, as said below
- score_multiplier: float32 [], replicated, may hold values from 90 to 110
- score_offset: float32 [], replicated, may hold values from -10.5 to -9.5
- objective_cotangent: float32 [], replicated, may hold values from 0.1 to 0.3
Outputs:
- picture_vector_derivative: float32 [8192, 1152], P('dp')
- caption_vector_derivative: float32 [8192, 1152], P('dp')
The draws below stay inside these ranges and needn't reach their ends.
Inputs may be any that keep to these rules, and one draw needn't show every extreme that they name: Each row matched_caption_index[p] is a permutation of 0 .. 511.
All inputs are finite; a program needn't handle non-finite values.
Results may differ from the reference program's by a relative error of at most 0.0045.
Values may be sent and summed in bfloat16 or wider, within the bound.
No kernel may reach another device: no remote copies, remote signals or barrier semaphores. Data moves between devices by JAX's collectives and lax.ppermute only.
A program may use at most 64 MiB of HBM per device.

```python
import jax
import jax.numpy as jnp
from jax import lax

FEATURE_DIM = 1152
COUPLES_PER_PART = 512
STEPS = 8
N_DP = 16


def pairing(key):
    keys = jax.random.split(jax.random.fold_in(key, 11), N_DP)
    return jax.vmap(lambda single: jax.random.permutation(single, COUPLES_PER_PART))(keys).astype(jnp.int32)


def embeddings(key):
    factor = (FEATURE_DIM * 1152.0) ** (-0.25)
    base = jax.random.normal(jax.random.fold_in(key, 21), (N_DP, COUPLES_PER_PART, FEATURE_DIM), jnp.float32) * factor
    return jnp.clip(base, -1.0, 1.0)


def draw_matched_caption_index(key, part):
    pairs = pairing(key)
    return pairs


def draw_picture_vectors(key, part):
    vectors = embeddings(key)
    return vectors.reshape(N_DP * COUPLES_PER_PART, FEATURE_DIM).astype(jnp.bfloat16)


def draw_caption_vectors(key, part):
    vectors = embeddings(key)
    pairs = pairing(key)
    key = jax.random.fold_in(key, 9)
    factor = (FEATURE_DIM * 1152.0) ** (-0.25)
    cosine = jax.random.uniform(jax.random.fold_in(key, 1), (N_DP, COUPLES_PER_PART, 1), jnp.float32, 0.1, 0.4)
    noise = jax.random.normal(jax.random.fold_in(key, 2), (N_DP, COUPLES_PER_PART, FEATURE_DIM), jnp.float32) * factor
    paired = cosine * vectors + jnp.sqrt(1.0 - cosine * cosine) * noise
    placed = jax.vmap(lambda block, order: jnp.zeros_like(block).at[order].set(block))(paired, pairs)
    return jnp.clip(placed, -1.0, 1.0).reshape(N_DP * COUPLES_PER_PART, FEATURE_DIM).astype(jnp.bfloat16)


def setup_inputs(seed: int = 0) -> dict:
    key_list = jax.random.split(jax.random.key(seed), 7)
    return {
        "picture_vectors": draw_picture_vectors(jax.random.fold_in(key_list[6], 71), 0),
        "caption_vectors": draw_caption_vectors(jax.random.fold_in(key_list[6], 71), 0),
        "matched_caption_index": draw_matched_caption_index(jax.random.fold_in(key_list[6], 71), 0),
        "score_multiplier": jnp.clip(jax.random.uniform(key_list[3], (), jnp.float32, 90.0, 110.0), 90.0, 110.0),
        "score_offset": jnp.clip(jax.random.uniform(key_list[4], (), jnp.float32, -10.5, -9.5), -10.5, -9.5),
        "objective_cotangent": jnp.clip(jax.random.uniform(key_list[5], (), jnp.float32, 0.1, 0.3), 0.1, 0.3),
    }


def reference(picture_vectors, caption_vectors, matched_caption_index, score_multiplier, score_offset, objective_cotangent):
    img = picture_vectors.reshape(N_DP, COUPLES_PER_PART, FEATURE_DIM).astype(jnp.float32)
    txt = caption_vectors.reshape(N_DP, COUPLES_PER_PART, FEATURE_DIM).astype(jnp.float32)
    column = lax.broadcasted_iota(jnp.int32, (N_DP, COUPLES_PER_PART, COUPLES_PER_PART), 2)
    match = (column == matched_caption_index[:, :, None]).astype(jnp.float32)
    picture_derivative_piece = jnp.zeros((N_DP, COUPLES_PER_PART, FEATURE_DIM), jnp.float32)
    caption_derivative_piece = jnp.zeros((N_DP, COUPLES_PER_PART, FEATURE_DIM), jnp.float32)
    for step in range(STEPS):
        moved = jnp.roll(txt, step, axis=0)
        inner_score_table = jnp.einsum('prd,pqd->prq', img, moved)
        couple_score_table = score_multiplier * inner_score_table + score_offset
        positive = 1.0 if step == 0 else 0.0
        grads = (objective_cotangent * (jax.nn.sigmoid(couple_score_table) - positive * match)).astype(jnp.bfloat16)
        grads_wide = grads.astype(jnp.float32)
        picture_derivative_piece = picture_derivative_piece + jnp.einsum('prq,pqd->prd', grads_wide, moved)
        contrib = jnp.einsum('prq,prd->pqd', grads_wide, img)
        caption_derivative_piece = caption_derivative_piece + jnp.roll(contrib, -step, axis=0)
    picture_vector_derivative = (score_multiplier * picture_derivative_piece).reshape(N_DP * COUPLES_PER_PART, FEATURE_DIM)
    caption_vector_derivative = (score_multiplier * caption_derivative_piece).reshape(N_DP * COUPLES_PER_PART, FEATURE_DIM)
    return picture_vector_derivative, caption_vector_derivative
```

```python
import jax
import jax.numpy as jnp
from jax import lax
from jax.experimental import pallas as pl
from jax.experimental.pallas import tpu as pltpu
from jax.sharding import PartitionSpec as P

GROUP = 4
CHUNKS = 2
VMEM_BYTES = 40 * 1024 * 1024

FIRST, CORE, SIDE = 0, 1, 2


def hop(x, pairs):
    return lax.ppermute(x, ("dp", "rep"), pairs)


def pairs_of(devices, target, members):
    pairs = []
    for p in range(devices):
        if p % GROUP in members:
            q = target(p)
            pairs.append((2 * p, 2 * q))
            pairs.append((2 * (devices - 1 - p) + 1, 2 * (devices - 1 - q) + 1))
    return pairs


def grads_of(scale_ref, left, block, match=None):
    product = lax.dot_general(
        left, block, (((1,), (1,)), ((), ())), preferred_element_type=jnp.float32
    )
    value = jax.nn.sigmoid(scale_ref[0] * product + scale_ref[1])
    if match is not None:
        value = value - match
    return (scale_ref[2] * value).astype(jnp.bfloat16)


def add_blocks(scale_ref, left_ref, refs, out_ref, match=None):
    left = left_ref[...]
    blocks = [ref[...] for ref in refs]
    grads = [grads_of(scale_ref, left, block, match) for block in blocks]
    if len(refs) > 1:
        blocks, grads = [jnp.concatenate(blocks, axis=0)], [jnp.concatenate(grads, axis=1)]
    out_ref[...] += jnp.dot(grads[0], blocks[0], preferred_element_type=jnp.float32)


def first_kernel(
    flag_ref, scale_ref, down_ref, along_ref, left_ref, own_ref, one_ref, out_ref
):
    own_rows = pl.program_id(0) == 0
    out_ref[...] = jnp.zeros_like(out_ref)

    @pl.when(own_rows)
    def _():
        shape = (left_ref.shape[0], own_ref.shape[0])
        column = lax.broadcasted_iota(jnp.int32, shape, 1)
        row = lax.broadcasted_iota(jnp.int32, shape, 0)
        straight = (column == down_ref[...]).astype(jnp.float32)
        turned = (row == along_ref[...]).astype(jnp.float32)
        match = jnp.where(flag_ref[FIRST] == 1, straight, turned)
        add_blocks(scale_ref, left_ref, [own_ref], out_ref, match)

    @pl.when(jnp.logical_and(jnp.logical_not(own_rows), flag_ref[CORE] == 0))
    def _():
        add_blocks(scale_ref, left_ref, [own_ref], out_ref)

    add_blocks(scale_ref, left_ref, [one_ref], out_ref)


def second_kernel(flag_ref, scale_ref, left_ref, sum_ref, one_ref, over_ref, out_ref):
    out_ref[...] = sum_ref[...]
    add_blocks(scale_ref, left_ref, [one_ref], out_ref)

    @pl.when(flag_ref[SIDE] == 1)
    def _():
        add_blocks(scale_ref, left_ref, [over_ref], out_ref)


def third_kernel(flag_ref, scale_ref, left_ref, sum_ref, *rest):
    two, over, last, out_ref = rest[:CHUNKS], rest[CHUNKS:-2], rest[-2], rest[-1]
    other_rows = pl.program_id(0) == 1
    out_ref[...] = sum_ref[...]

    @pl.when(jnp.logical_or(other_rows, flag_ref[CORE] == 0))
    def _():
        add_blocks(scale_ref, left_ref, two, out_ref)

    @pl.when(flag_ref[CORE] == 1)
    def _():
        add_blocks(scale_ref, left_ref, over, out_ref)

    @pl.when(flag_ref[SIDE] == 0)
    def _():
        add_blocks(scale_ref, left_ref, [last], out_ref)


def last_kernel(flag_ref, scale_ref, left_ref, sum_ref, last_ref, out_ref, total_ref):
    total_ref[...] = sum_ref[...]

    @pl.when(flag_ref[SIDE] == 0)
    def _():
        add_blocks(scale_ref, left_ref, [last_ref], total_ref)

    out_ref[...] = total_ref[...].astype(out_ref.dtype)


def whole(x):
    return pl.BlockSpec(x.shape, lambda i: (0,) * x.ndim)


def params():
    return pltpu.CompilerParams(
        dimension_semantics=("arbitrary",), vmem_limit_bytes=VMEM_BYTES
    )


def cost(pairs, rows, depth):
    return pl.CostEstimate(
        flops=int(4 * pairs * rows * rows * depth),
        bytes_accessed=int(8 * rows * depth),
        transcendentals=int(pairs * rows * rows),
    )


SMEM = pl.BlockSpec(memory_space=pltpu.SMEM)


def per_device(
    picture_vectors,
    caption_vectors,
    matched_caption_index,
    score_multiplier,
    score_offset,
    objective_cotangent,
):
    rows, depth = picture_vectors.shape
    devices = lax.axis_size("dp")
    first = lax.axis_index("rep") == 0
    place = lax.axis_index("dp")
    place = jnp.where(first, place, devices - 1 - place)
    flags = jnp.stack([first.astype(jnp.int32), place & 1, (place >> 1) & 1])
    scale = jnp.stack([score_multiplier, score_offset, objective_cotangent])

    def up(p):
        return (p + GROUP) % devices

    def across(p):
        return p ^ 2

    def swapped(p):
        return p ^ 1

    to_up = pairs_of(devices, up, (0, 1, 2, 3))
    to_side_1 = pairs_of(devices, across, (0, 1))
    core_1_across = pairs_of(devices, across, (1, 3))
    onward = pairs_of(devices, up, (1, 3)) + pairs_of(devices, across, (0, 2))
    last_step = pairs_of(devices, up, (0,)) + pairs_of(devices, across, (3,))
    core_swap = pairs_of(devices, swapped, (0, 1, 2, 3))
    replica_swap = [(2 * p + r, 2 * p + 1 - r) for p in range(devices) for r in range(2)]

    moving = jnp.where(first, caption_vectors, picture_vectors)
    fixed = jnp.where(first, picture_vectors, caption_vectors)
    size = rows // CHUNKS
    own = [moving[k * size : (k + 1) * size] for k in range(CHUNKS)]

    tile = pl.BlockSpec((rows, depth), lambda i: (i, 0))
    down = matched_caption_index.reshape(rows, 1)
    sums = jax.ShapeDtypeStruct((2 * rows, depth), jnp.float32)

    def kernel(body, name, pairs, operands, specs):
        return pl.pallas_call(
            body,
            grid=(2,),
            out_shape=sums,
            in_specs=[SMEM, SMEM] + specs,
            out_specs=tile,
            compiler_params=params(),
            cost_estimate=cost(pairs, rows, depth),
            name=name,
        )(flags, scale, *operands)

    one = [hop(x, to_up) for x in own]
    other_fixed = hop(fixed, core_swap)
    from_0 = hop(moving, to_side_1)
    both = jnp.concatenate([fixed, other_fixed], axis=0)
    two_a = hop(one[0], onward)
    over_a = hop(one[0], core_1_across)
    total = kernel(
        first_kernel,
        "first_blocks",
        3,
        (down, matched_caption_index, both, moving, one[0]),
        [whole(down), whole(matched_caption_index), tile, whole(moving), whole(one[0])],
    )
    one_b, total = lax.optimization_barrier((one[1], total))
    two_b = hop(one_b, onward)
    over_b = hop(one_b, core_1_across)
    total = kernel(
        second_kernel,
        "second_blocks",
        3,
        (both, total, one_b, from_0),
        [tile, tile, whole(one_b), whole(from_0)],
    )
    last_a = hop(two_a, last_step)
    two_b, total = lax.optimization_barrier((two_b, total))
    last_b = hop(two_b, last_step)
    blocks = [two_a, two_b, over_a, over_b, last_a]
    total = kernel(
        third_kernel,
        "third_blocks",
        4,
        (both, total, *blocks),
        [tile, tile] + [whole(x) for x in blocks],
    )

    def finish(which, dtype, name):
        part = pl.BlockSpec((rows, depth), lambda i: (which, 0))
        return pl.pallas_call(
            last_kernel,
            grid=(1,),
            out_shape=jax.ShapeDtypeStruct((rows, depth), dtype),
            in_specs=[SMEM, SMEM, part, part, whole(last_b)],
            out_specs=tile,
            scratch_shapes=[pltpu.VMEM((rows, depth), jnp.float32)],
            compiler_params=params(),
            cost_estimate=cost(0.5, rows, depth),
            name=name,
        )(flags, scale, both, total, last_b)

    other_total = finish(1, jnp.bfloat16, "last_block_other")
    received = hop(other_total, core_swap)
    own_total = finish(0, jnp.float32, "last_block_own")

    mine = (score_multiplier * (own_total + received.astype(jnp.float32))).astype(jnp.bfloat16)
    theirs = hop(mine, replica_swap)
    return (
        jnp.where(first, mine, theirs).astype(jnp.float32),
        jnp.where(first, theirs, mine).astype(jnp.float32),
    )


def solution(mesh):
    placed = (P("dp", None), P("dp", None), P("dp", None), P(), P(), P())
    return jax.shard_map(
        per_device,
        mesh=mesh,
        in_specs=placed,
        out_specs=(P("dp", None), P("dp", None)),
        check_vma=False,
    )
```

```python
import jax
import jax.numpy as jnp
from jax import lax
from jax.experimental import pallas as pl
from jax.experimental.pallas import tpu as pltpu
from jax.sharding import PartitionSpec as P

GROUP = 4
CHUNKS = 2
VMEM_BYTES = 40 * 1024 * 1024

FIRST, CORE, SIDE = 0, 1, 2


def hop(x, pairs):
    return lax.ppermute(x, ("dp", "rep"), pairs)


def pairs_of(devices, target, members):
    pairs = []
    for p in range(devices):
        if p % GROUP in members:
            q = target(p)
            pairs.append((2 * p, 2 * q))
            pairs.append((2 * (devices - 1 - p) + 1, 2 * (devices - 1 - q) + 1))
    return pairs


def grads_of(scale_ref, left, block, match=None):
    product = lax.dot_general(
        left, block, (((1,), (1,)), ((), ())), preferred_element_type=jnp.float32
    )
    value = 1.0 / (scale_ref[2] + jnp.exp2(scale_ref[0] * product + scale_ref[1]))
    if match is not None:
        value = value - scale_ref[3] * match
    return value.astype(jnp.bfloat16)


def add_blocks(scale_ref, left_ref, refs, out_ref, match=None):
    left = left_ref[...]
    blocks = [ref[...] for ref in refs]
    size = blocks[0].shape[0]
    grads = [
        grads_of(
            scale_ref, left, block, None if match is None else match[:, k * size : (k + 1) * size]
        )
        for k, block in enumerate(blocks)
    ]
    if len(refs) > 1:
        blocks, grads = [jnp.concatenate(blocks, axis=0)], [jnp.concatenate(grads, axis=1)]
    out_ref[...] += jnp.dot(grads[0], blocks[0], preferred_element_type=jnp.float32)


def first_kernel(
    flag_ref,
    scale_ref,
    down_ref,
    along_ref,
    left_ref,
    own_a_ref,
    own_b_ref,
    one_ref,
    from_ref,
    out_ref,
):
    own_rows = pl.program_id(0) == 0
    own_refs = [own_a_ref, own_b_ref]
    out_ref[...] = jnp.zeros_like(out_ref)

    @pl.when(own_rows)
    def _():
        shape = (left_ref.shape[0], along_ref.shape[1])
        column = lax.broadcasted_iota(jnp.int32, shape, 1)
        row = lax.broadcasted_iota(jnp.int32, shape, 0)
        straight = (column == down_ref[...]).astype(jnp.float32)
        turned = (row == along_ref[...]).astype(jnp.float32)
        match = jnp.where(flag_ref[FIRST] == 1, straight, turned)
        add_blocks(scale_ref, left_ref, own_refs, out_ref, match)

    @pl.when(jnp.logical_and(jnp.logical_not(own_rows), flag_ref[CORE] == 0))
    def _():
        add_blocks(scale_ref, left_ref, own_refs, out_ref)

    add_blocks(scale_ref, left_ref, [one_ref], out_ref)

    @pl.when(flag_ref[SIDE] == 1)
    def _():
        add_blocks(scale_ref, left_ref, [from_ref], out_ref)


def brought(flag_ref):
    over = jnp.logical_or(flag_ref[CORE] == 1, flag_ref[SIDE] == 1)
    return over, flag_ref[SIDE] == 0


def second_kernel(flag_ref, scale_ref, left_ref, sum_ref, one_ref, over_ref, out_ref):
    has_over, _ = brought(flag_ref)
    out_ref[...] = sum_ref[...]
    add_blocks(scale_ref, left_ref, [one_ref], out_ref)

    @pl.when(has_over)
    def _():
        add_blocks(scale_ref, left_ref, [over_ref], out_ref)


def third_kernel(
    flag_ref, scale_ref, left_ref, sum_ref, two_a, two_b, from_b, last, out_ref
):
    other_rows = pl.program_id(0) == 1
    core, side = flag_ref[CORE], flag_ref[SIDE]
    out_ref[...] = sum_ref[...]

    @pl.when(jnp.logical_or(jnp.logical_and(core == 1, other_rows), core + side == 0))
    def _():
        add_blocks(scale_ref, left_ref, [two_a, two_b], out_ref)

    @pl.when(side == 1)
    def _():
        add_blocks(scale_ref, left_ref, [from_b], out_ref)

    @pl.when(side == 0)
    def _():
        add_blocks(scale_ref, left_ref, [last], out_ref)


def last_kernel(flag_ref, scale_ref, left_ref, sum_ref, over, last, out_ref, total_ref):
    has_over, has_last = brought(flag_ref)
    total_ref[...] = sum_ref[...]

    @pl.when(has_over)
    def _():
        add_blocks(scale_ref, left_ref, [over], total_ref)

    @pl.when(has_last)
    def _():
        add_blocks(scale_ref, left_ref, [last], total_ref)

    out_ref[...] = total_ref[...].astype(out_ref.dtype)


def whole(x):
    return pl.BlockSpec(x.shape, lambda i: (0,) * x.ndim)


def params():
    return pltpu.CompilerParams(
        dimension_semantics=("arbitrary",), vmem_limit_bytes=VMEM_BYTES
    )


def cost(pairs, rows, depth):
    return pl.CostEstimate(
        flops=int(4 * pairs * rows * rows * depth),
        bytes_accessed=int(8 * rows * depth),
        transcendentals=int(pairs * rows * rows),
    )


SMEM = pl.BlockSpec(memory_space=pltpu.SMEM)


def per_device(
    picture_vectors,
    caption_vectors,
    matched_caption_index,
    score_multiplier,
    score_offset,
    objective_cotangent,
):
    rows, depth = picture_vectors.shape
    devices = lax.axis_size("dp")
    first = lax.axis_index("rep") == 0
    place = lax.axis_index("dp")
    place = jnp.where(first, place, devices - 1 - place)
    flags = jnp.stack([first.astype(jnp.int32), place & 1, (place >> 1) & 1])
    log2e = 1.4426950408889634
    scale = jnp.stack(
        [
            -log2e * score_multiplier,
            -log2e * score_offset - jnp.log2(objective_cotangent),
            1.0 / objective_cotangent,
            objective_cotangent,
        ]
    )

    def up(p):
        return (p + GROUP) % devices

    def across(p):
        return p ^ 2

    def swapped(p):
        return p ^ 1

    to_up = pairs_of(devices, up, (0, 1, 2, 3))
    to_side_1 = pairs_of(devices, across, (0, 1))
    but_2_across = pairs_of(devices, across, (0, 1, 3))
    onward = pairs_of(devices, up, (1, 3)) + pairs_of(devices, across, (2,))
    last_step = pairs_of(devices, up, (0,)) + pairs_of(devices, across, (3,))
    core_swap = pairs_of(devices, swapped, (0, 1, 2, 3))
    replica_swap = [(2 * p + r, 2 * p + 1 - r) for p in range(devices) for r in range(2)]

    size = rows // CHUNKS
    parts = [slice(k * size, (k + 1) * size) for k in range(CHUNKS)]
    own = [jnp.where(first, caption_vectors[x], picture_vectors[x]) for x in parts]
    *own, texts, images = lax.optimization_barrier((*own, caption_vectors, picture_vectors))
    fixed = jnp.where(first, images, texts)

    tile = pl.BlockSpec((rows, depth), lambda i: (i, 0))
    down = matched_caption_index.reshape(rows, 1)

    def kernel(body, name, operands, specs, steps=2):
        return pl.pallas_call(
            body,
            grid=(steps,),
            out_shape=jax.ShapeDtypeStruct((steps * rows, depth), jnp.float32),
            in_specs=[SMEM, SMEM] + specs + [whole(x) for x in operands[len(specs) :]],
            out_specs=tile,
            compiler_params=params(),
            cost_estimate=pl.CostEstimate(flops=1, bytes_accessed=1, transcendentals=0),
            name=name,
        )(flags, scale, *operands)

    one_a, one_b = [hop(x, to_up) for x in own]
    from_a = hop(own[0], to_side_1)
    other_fixed = hop(fixed, core_swap)
    both = jnp.concatenate([fixed, other_fixed], axis=0)
    two_a = hop(one_a, onward)
    over_a = hop(one_a, but_2_across)
    total = kernel(
        first_kernel,
        "first_blocks",
        (down, matched_caption_index, both, *own, one_a, from_a),
        [whole(down), whole(matched_caption_index), tile],
    )
    one_b, own_b, total = lax.optimization_barrier((one_b, own[1], total))
    two_b = hop(one_b, onward)
    from_b = hop(own_b, to_side_1)
    total = kernel(
        second_kernel, "second_blocks", (both, total, one_b, over_a), [tile, tile]
    )
    last_a = hop(two_a, last_step)
    two_b, one_b, total = lax.optimization_barrier((two_b, one_b, total))
    last_b = hop(two_b, last_step)
    over_b = hop(one_b, but_2_across)
    total = kernel(
        third_kernel,
        "third_blocks",
        (both, total, two_a, two_b, from_b, last_a),
        [tile, tile],
    )

    def finish(which, dtype, name):
        part = pl.BlockSpec((rows, depth), lambda i: (which, 0))
        return pl.pallas_call(
            last_kernel,
            grid=(1,),
            out_shape=jax.ShapeDtypeStruct((rows, depth), dtype),
            in_specs=[SMEM, SMEM, part, part, whole(over_b), whole(last_b)],
            out_specs=tile,
            scratch_shapes=[pltpu.VMEM((rows, depth), jnp.float32)],
            compiler_params=params(),
            cost_estimate=cost(0.5, rows, depth),
            name=name,
        )(flags, scale, both, total, over_b, last_b)

    other_total = finish(1, jnp.bfloat16, "last_block_other")
    received = hop(other_total, core_swap)
    own_total = finish(0, jnp.float32, "last_block_own")

    mine = (score_multiplier * (own_total + received.astype(jnp.float32))).astype(jnp.bfloat16)
    theirs = hop(mine, replica_swap)
    return (
        jnp.where(first, mine, theirs).astype(jnp.float32),
        jnp.where(first, theirs, mine).astype(jnp.float32),
    )


def solution(mesh):
    placed = (P("dp", None), P("dp", None), P("dp", None), P(), P(), P())
    return jax.shard_map(
        per_device,
        mesh=mesh,
        in_specs=placed,
        out_specs=(P("dp", None), P("dp", None)),
        check_vma=False,
    )
```

```python
import jax
import jax.numpy as jnp
from jax import lax
from jax.experimental import pallas as pl
from jax.experimental.pallas import tpu as pltpu
from jax.sharding import PartitionSpec as P

GROUP = 4
VMEM_BYTES = 36 * 1024 * 1024
NO_ROOM = 60 * 1024 * 1024

FIRST, CORE, SIDE = 0, 1, 2


def hop(x, pairs):
    return lax.ppermute(x, ("dp", "rep"), pairs)


def pairs_of(devices, target, members):
    pairs = []
    for p in range(devices):
        if p % GROUP in members:
            q = target(p)
            pairs.append((2 * p, 2 * q))
            pairs.append((2 * (devices - 1 - p) + 1, 2 * (devices - 1 - q) + 1))
    return pairs


def grads_of(scale_ref, left, block, match=None):
    product = lax.dot_general(
        left, block, (((1,), (1,)), ((), ())), preferred_element_type=jnp.float32
    )
    value = 1.0 / (scale_ref[2] + jnp.exp2(scale_ref[0] * product + scale_ref[1]))
    if match is not None:
        value = value - scale_ref[3] * match
    return value.astype(jnp.bfloat16)


def add_block(scale_ref, left_ref, refs, out_ref, match=None):
    block = jnp.concatenate([ref[...] for ref in refs], axis=0) if len(refs) > 1 else refs[0][...]
    grads = grads_of(scale_ref, left_ref[...], block, match)
    out_ref[...] += jnp.dot(grads, block, preferred_element_type=jnp.float32)


def pick_kernel(image_ref, text_ref, own_a_ref, own_b_ref, fixed_ref, sems):
    half = own_a_ref.shape[0]

    def copies(moving_ref, still_ref):
        moves = [
            pltpu.make_async_copy(moving_ref.at[:half], own_a_ref, sems.at[0]),
            pltpu.make_async_copy(moving_ref.at[half:], own_b_ref, sems.at[1]),
            pltpu.make_async_copy(still_ref, fixed_ref, sems.at[2]),
        ]
        for move in moves:
            move.start()
        for move in moves:
            move.wait()

    first = lax.axis_index("rep") == 0

    @pl.when(first)
    def _():
        copies(text_ref, image_ref)

    @pl.when(jnp.logical_not(first))
    def _():
        copies(image_ref, text_ref)


def choose_rows(fixed_ref, other_ref, left_ref):
    @pl.when(pl.program_id(0) == 0)
    def _():
        left_ref[...] = fixed_ref[...]

    @pl.when(pl.program_id(0) == 1)
    def _():
        left_ref[...] = other_ref[...]


def own_kernel(
    flag_ref, scale_ref, down_ref, along_ref, left_ref, own_a_ref, own_b_ref, out_ref
):
    shape = (left_ref.shape[0], along_ref.shape[1])
    column = lax.broadcasted_iota(jnp.int32, shape, 1)
    row = lax.broadcasted_iota(jnp.int32, shape, 0)
    straight = (column == down_ref[...]).astype(jnp.float32)
    turned = (row == along_ref[...]).astype(jnp.float32)
    match = jnp.where(flag_ref[FIRST] == 1, straight, turned)
    out_ref[...] = jnp.zeros_like(out_ref)
    add_block(scale_ref, left_ref, [own_a_ref, own_b_ref], out_ref, match)


def second_kernel(
    flag_ref,
    scale_ref,
    sum_ref,
    fixed_ref,
    other_ref,
    own_a,
    own_b,
    one_a,
    one_b,
    group,
    over,
    out_ref,
    left_ref,
):
    other_rows = pl.program_id(0) == 1
    core, side = flag_ref[CORE], flag_ref[SIDE]
    choose_rows(fixed_ref, other_ref, left_ref)

    @pl.when(other_rows)
    def _():
        out_ref[...] = jnp.zeros_like(out_ref)

    @pl.when(jnp.logical_not(other_rows))
    def _():
        out_ref[...] = sum_ref[...]

    @pl.when(jnp.logical_and(other_rows, core == 0))
    def _():
        add_block(scale_ref, left_ref, [own_a, own_b], out_ref)

    add_block(scale_ref, left_ref, [one_a, one_b], out_ref)

    @pl.when(jnp.logical_or(core == 1, side == 1))
    def _():
        add_block(scale_ref, left_ref, [group, over], out_ref)


def third_kernel(
    flag_ref, scale_ref, sum_ref, fixed_ref, other_ref, two_a, two_b, over, last, out_ref, left_ref
):
    other_rows = pl.program_id(0) == 1
    core, side = flag_ref[CORE], flag_ref[SIDE]
    choose_rows(fixed_ref, other_ref, left_ref)
    out_ref[...] = sum_ref[...]

    @pl.when(jnp.logical_or(jnp.logical_and(core == 1, other_rows), core + side == 0))
    def _():
        add_block(scale_ref, left_ref, [two_a, two_b], out_ref)

    add_block(scale_ref, left_ref, [over, last], out_ref)


def last_kernel(flag_ref, scale_ref, left_ref, sum_ref, group, last, out_ref, total_ref):
    total_ref[...] = sum_ref[...]

    @pl.when(flag_ref[SIDE] == 0)
    def _():
        add_block(scale_ref, left_ref, [last], total_ref)

    @pl.when(flag_ref[SIDE] == 1)
    def _():
        add_block(scale_ref, left_ref, [group], total_ref)

    out_ref[...] = total_ref[...].astype(out_ref.dtype)


def whole(x):
    return pl.BlockSpec(x.shape, lambda i: (0,) * x.ndim)


def params():
    return pltpu.CompilerParams(
        dimension_semantics=("arbitrary",), vmem_limit_bytes=VMEM_BYTES
    )


NO_COST = pl.CostEstimate(flops=1, bytes_accessed=1, transcendentals=0)
SMEM = pl.BlockSpec(memory_space=pltpu.SMEM)
ANY = pl.BlockSpec(memory_space=pl.ANY)


def per_device(
    picture_vectors,
    caption_vectors,
    matched_caption_index,
    score_multiplier,
    score_offset,
    objective_cotangent,
):
    rows, depth = picture_vectors.shape
    devices = lax.axis_size("dp")
    first = lax.axis_index("rep") == 0
    place = lax.axis_index("dp")
    place = jnp.where(first, place, devices - 1 - place)
    flags = jnp.stack([first.astype(jnp.int32), place & 1, (place >> 1) & 1])
    log2e = 1.4426950408889634
    scale = jnp.stack(
        [
            -log2e * score_multiplier,
            -log2e * score_offset - jnp.log2(objective_cotangent),
            1.0 / objective_cotangent,
            objective_cotangent,
        ]
    )

    def up(p):
        return (p + GROUP) % devices

    def across(p):
        return p ^ 2

    def swapped(p):
        return p ^ 1

    to_up = pairs_of(devices, up, (0, 1, 2, 3))
    to_side_1 = pairs_of(devices, across, (0, 1))
    but_2_across = pairs_of(devices, across, (0, 1, 3))
    onward = pairs_of(devices, up, (1, 3)) + pairs_of(devices, across, (2,))
    last_step = pairs_of(devices, up, (0,)) + pairs_of(devices, across, (3,))
    core_swap = pairs_of(devices, swapped, (0, 1, 2, 3))
    replica_swap = [(2 * p + r, 2 * p + 1 - r) for p in range(devices) for r in range(2)]

    kind = picture_vectors.dtype
    half_shape = jax.ShapeDtypeStruct((rows // 2, depth), kind)
    full_shape = jax.ShapeDtypeStruct((rows, depth), kind)
    own_a, own_b, fixed = pl.pallas_call(
        pick_kernel,
        out_shape=[half_shape, half_shape, full_shape],
        in_specs=[ANY, ANY],
        out_specs=[pl.BlockSpec(memory_space=pltpu.VMEM)] * 3,
        scratch_shapes=[pltpu.SemaphoreType.DMA((3,))],
        compiler_params=pltpu.CompilerParams(vmem_limit_bytes=NO_ROOM),
        cost_estimate=NO_COST,
        name="pick",
    )(picture_vectors, caption_vectors)

    tile = pl.BlockSpec((rows, depth), lambda i: (i, 0))
    down = matched_caption_index.reshape(rows, 1)

    def kernel(body, name, operands, specs, steps=2):
        return pl.pallas_call(
            body,
            grid=(steps,),
            out_shape=jax.ShapeDtypeStruct((steps * rows, depth), jnp.float32),
            in_specs=[SMEM, SMEM] + specs + [whole(x) for x in operands[len(specs) :]],
            out_specs=tile,
            scratch_shapes=[pltpu.VMEM((rows, depth), kind)] * (steps - 1),
            compiler_params=params(),
            cost_estimate=NO_COST,
            name=name,
        )(flags, scale, *operands)

    one_a, one_b = hop(own_a, to_up), hop(own_b, to_up)
    group_a = hop(own_a, to_side_1)
    other_fixed = hop(fixed, core_swap)
    one_a, fixed_late = lax.optimization_barrier((one_a, fixed))
    two_a = hop(one_a, onward)
    over_a = hop(one_a, but_2_across)
    total = kernel(
        own_kernel, "own_pairs", (down, matched_caption_index, fixed_late, own_a, own_b), [], steps=1
    )
    one_b, total = lax.optimization_barrier((one_b, total))
    two_b = hop(one_b, onward)
    over_b = hop(one_b, but_2_across)
    two_a, total = lax.optimization_barrier((two_a, total))
    total = kernel(
        second_kernel,
        "second_blocks",
        (total, fixed, other_fixed, own_a, own_b, one_a, one_b, group_a, over_a),
        [],
    )
    last_a = hop(two_a, last_step)
    two_b, own_b, total = lax.optimization_barrier((two_b, own_b, total))
    last_b = hop(two_b, last_step)
    group_b = hop(own_b, to_side_1)
    total = kernel(
        third_kernel,
        "third_blocks",
        (total, fixed, other_fixed, two_a, two_b, over_b, last_a),
        [tile],
    )

    def finish(which, left, dtype, name):
        part = pl.BlockSpec((rows, depth), lambda i: (which, 0))
        return pl.pallas_call(
            last_kernel,
            grid=(1,),
            out_shape=jax.ShapeDtypeStruct((rows, depth), dtype),
            in_specs=[SMEM, SMEM, whole(left), part, whole(group_b), whole(last_b)],
            out_specs=tile,
            scratch_shapes=[pltpu.VMEM((rows, depth), jnp.float32)],
            compiler_params=params(),
            cost_estimate=NO_COST,
            name=name,
        )(flags, scale, left, total, group_b, last_b)

    other_total = finish(1, other_fixed, jnp.bfloat16, "last_block_other")
    received = hop(other_total, core_swap)
    own_total = finish(0, fixed, jnp.float32, "last_block_own")

    mine = (score_multiplier * (own_total + received.astype(jnp.float32))).astype(jnp.bfloat16)
    theirs = hop(mine, replica_swap)
    return (
        jnp.where(first, mine, theirs).astype(jnp.float32),
        jnp.where(first, theirs, mine).astype(jnp.float32),
    )


def solution(mesh):
    placed = (P("dp", None), P("dp", None), P("dp", None), P(), P(), P())
    return jax.shard_map(
        per_device,
        mesh=mesh,
        in_specs=placed,
        out_specs=(P("dp", None), P("dp", None)),
        check_vma=False,
    )
```

```python
import functools

import jax
import jax.numpy as jnp
from jax import lax
from jax.experimental import pallas as pl
from jax.experimental.pallas import tpu as pltpu
from jax.sharding import PartitionSpec as P

GROUP = 4
VMEM_BYTES = 36 * 1024 * 1024
NO_ROOM = 60 * 1024 * 1024
PICK_BYTES = NO_ROOM

FIRST, CORE, SIDE = 0, 1, 2


def hop(x, pairs):
    return lax.ppermute(x, ("dp", "rep"), pairs)


def pairs_of(devices, target, members):
    pairs = []
    for p in range(devices):
        if p % GROUP in members:
            q = target(p)
            pairs.append((2 * p, 2 * q))
            pairs.append((2 * (devices - 1 - p) + 1, 2 * (devices - 1 - q) + 1))
    return pairs


def grads_of(scale_ref, left, block, match=None):
    product = lax.dot_general(
        left, block, (((1,), (1,)), ((), ())), preferred_element_type=jnp.float32
    )
    value = 1.0 / (scale_ref[2] + jnp.exp2(scale_ref[0] * product + scale_ref[1]))
    if match is not None:
        value = value - scale_ref[3] * match
    return value.astype(jnp.bfloat16)


def add_block(scale_ref, left_ref, refs, out_ref, match=None, fresh=False):
    block = jnp.concatenate([ref[...] for ref in refs], axis=0) if len(refs) > 1 else refs[0][...]
    grads = grads_of(scale_ref, left_ref[...], block, match)
    part = jnp.dot(grads, block, preferred_element_type=jnp.float32)
    out_ref[...] = part if fresh else out_ref[...] + part


PIECES = 4


def copy_all(pairs, sems):
    moves = []
    for source, target in pairs:
        size = source.shape[0] // PIECES
        for k in range(PIECES):
            part = pl.ds(k * size, size)
            moves.append(
                pltpu.make_async_copy(source.at[part], target.at[part], sems.at[len(moves)])
            )
    for move in moves:
        move.start()
    for move in moves:
        move.wait()


def pick_first_kernel(image_ref, text_ref, own_a_ref, sems):
    part = pl.ds(0, own_a_ref.shape[0])
    first = lax.axis_index("rep") == 0

    @pl.when(first)
    def _():
        copy_all([(text_ref.at[part], own_a_ref)], sems)

    @pl.when(jnp.logical_not(first))
    def _():
        copy_all([(image_ref.at[part], own_a_ref)], sems)


def pick_rest_kernel(image_ref, text_ref, own_a_ref, own_b_ref, fixed_ref, sems):
    part = pl.ds(own_b_ref.shape[0], own_b_ref.shape[0])
    first = lax.axis_index("rep") == 0

    @pl.when(first)
    def _():
        copy_all([(text_ref.at[part], own_b_ref), (image_ref, fixed_ref)], sems)

    @pl.when(jnp.logical_not(first))
    def _():
        copy_all([(image_ref.at[part], own_b_ref), (text_ref, fixed_ref)], sems)


def write_kernel(picture_step, start, count, *refs):
    value_refs = refs[:count]
    picture_ref, caption_ref, wide_ref, sems = refs[-4:]
    to_picture = (lax.axis_index("rep") == 0) == picture_step
    size = value_refs[0].shape[0] // PIECES

    def write(target):
        moves = []
        for value_ref in value_refs:
            for k in range(PIECES):
                place = pl.ds(len(moves) * size, size)
                wide_ref[place] = value_ref[pl.ds(k * size, size)].astype(jnp.float32)
                there = target.at[pl.ds(start + len(moves) * size, size)]
                moves.append(
                    pltpu.make_async_copy(wide_ref.at[place], there, sems.at[len(moves)])
                )
                moves[-1].start()
        for move in moves:
            move.wait()

    @pl.when(to_picture)
    def _():
        write(picture_ref)

    @pl.when(jnp.logical_not(to_picture))
    def _():
        write(caption_ref)


def halves(total_ref):
    rows = total_ref.shape[0] // 2
    return total_ref.at[pl.ds(0, rows)], total_ref.at[pl.ds(rows, rows)]


def own_kernel(flag_ref, scale_ref, down_ref, along_ref, fixed_ref, own_a, own_b, total_ref):
    mine, others = halves(total_ref)
    shape = (fixed_ref.shape[0], along_ref.shape[1])
    column = lax.broadcasted_iota(jnp.int32, shape, 1)
    row = lax.broadcasted_iota(jnp.int32, shape, 0)
    straight = (column == down_ref[...]).astype(jnp.float32)
    turned = (row == along_ref[...]).astype(jnp.float32)
    match = jnp.where(flag_ref[FIRST] == 1, straight, turned)
    add_block(scale_ref, fixed_ref, [own_a, own_b], mine, match, fresh=True)
    others[...] = jnp.zeros_like(others)


def halves_kernel(flag_ref, scale_ref, _, fixed_ref, other_ref, half_ref, group_ref, total_ref):
    mine, others = halves(total_ref)
    add_block(scale_ref, fixed_ref, [half_ref, group_ref], mine)
    add_block(scale_ref, other_ref, [half_ref, group_ref], others)


def first_halves_kernel(
    flag_ref, scale_ref, _, fixed_ref, other_ref, half_ref, group_ref, own_a, own_b, total_ref
):
    halves_kernel(flag_ref, scale_ref, _, fixed_ref, other_ref, half_ref, group_ref, total_ref)

    @pl.when(flag_ref[CORE] == 0)
    def _():
        add_block(scale_ref, other_ref, [own_a, own_b], halves(total_ref)[1])


def two_kernel(flag_ref, scale_ref, _, fixed_ref, other_ref, two_a, two_b, total_ref):
    mine, others = halves(total_ref)
    core, side = flag_ref[CORE], flag_ref[SIDE]

    @pl.when(core + side == 0)
    def _():
        add_block(scale_ref, fixed_ref, [two_a, two_b], mine)

    @pl.when(jnp.logical_or(core == 1, side == 0))
    def _():
        add_block(scale_ref, other_ref, [two_a, two_b], others)


def last_sum(flag_ref, scale_ref, rows_ref, sum_ref, group_ref, last_ref, total_ref):
    total_ref[...] = sum_ref[...]

    @pl.when(flag_ref[SIDE] == 0)
    def _():
        add_block(scale_ref, rows_ref, [last_ref], total_ref)

    @pl.when(flag_ref[SIDE] == 1)
    def _():
        add_block(scale_ref, rows_ref, [group_ref], total_ref)


def last_other_kernel(
    start, flag_ref, scale_ref, sum_ref, other_ref, group_ref, last_ref, out_ref, total_ref
):
    part = pl.ds(start, out_ref.shape[0])
    rows_ref, sums_ref = other_ref.at[part], halves(sum_ref)[1].at[part]
    last_sum(flag_ref, scale_ref, rows_ref, sums_ref, group_ref, last_ref, total_ref)
    out_ref[...] = total_ref[...].astype(out_ref.dtype)


def last_own_kernel(
    start, flag_ref, scale_ref, sum_ref, fixed_ref, group_ref, last_ref, came_ref, out_ref, total_ref
):
    part = pl.ds(start, out_ref.shape[0])
    rows_ref, sums_ref = fixed_ref.at[part], halves(sum_ref)[0].at[part]
    last_sum(flag_ref, scale_ref, rows_ref, sums_ref, group_ref, last_ref, total_ref)
    whole_sum = total_ref[...] + came_ref[...].astype(jnp.float32)
    out_ref[...] = (scale_ref[4] * whole_sum).astype(out_ref.dtype)


def params():
    return pltpu.CompilerParams(vmem_limit_bytes=VMEM_BYTES)


NO_COST = pl.CostEstimate(flops=1, bytes_accessed=1, transcendentals=0)
SMEM = pl.BlockSpec(memory_space=pltpu.SMEM)
ANY = pl.BlockSpec(memory_space=pl.ANY)


def per_device(
    picture_vectors,
    caption_vectors,
    matched_caption_index,
    score_multiplier,
    score_offset,
    objective_cotangent,
):
    rows, depth = picture_vectors.shape
    devices = lax.axis_size("dp")
    first = lax.axis_index("rep") == 0
    place = lax.axis_index("dp")
    place = jnp.where(first, place, devices - 1 - place)
    flags = jnp.stack([first.astype(jnp.int32), place & 1, (place >> 1) & 1])
    log2e = 1.4426950408889634
    scale = jnp.stack(
        [
            -log2e * score_multiplier,
            -log2e * score_offset - jnp.log2(objective_cotangent),
            1.0 / objective_cotangent,
            objective_cotangent,
            score_multiplier,
        ]
    )

    def up(p):
        return (p + GROUP) % devices

    def across(p):
        return p ^ 2

    def swapped(p):
        return p ^ 1

    to_up = pairs_of(devices, up, (0, 1, 2, 3))
    to_side_1 = pairs_of(devices, across, (0, 1))
    but_2_across = pairs_of(devices, across, (0, 1, 3))
    onward = pairs_of(devices, up, (1, 3)) + pairs_of(devices, across, (2,))
    last_step = pairs_of(devices, up, (0,)) + pairs_of(devices, across, (3,))
    core_swap = pairs_of(devices, swapped, (0, 1, 2, 3))
    replica_swap = [(2 * p + r, 2 * p + 1 - r) for p in range(devices) for r in range(2)]

    kind = picture_vectors.dtype
    half = rows // 2
    half_shape = jax.ShapeDtypeStruct((half, depth), kind)
    full_shape = jax.ShapeDtypeStruct((rows, depth), kind)
    vmem = pl.BlockSpec(memory_space=pltpu.VMEM)
    arrays = (picture_vectors, caption_vectors)
    own_a = pl.pallas_call(
        pick_first_kernel,
        out_shape=half_shape,
        in_specs=[ANY, ANY],
        out_specs=vmem,
        scratch_shapes=[pltpu.SemaphoreType.DMA((PIECES,))],
        compiler_params=pltpu.CompilerParams(vmem_limit_bytes=PICK_BYTES),
        cost_estimate=NO_COST,
        name="pick_first",
    )(*arrays)
    own_b, fixed = pl.pallas_call(
        pick_rest_kernel,
        out_shape=[half_shape, full_shape],
        in_specs=[ANY, ANY, ANY],
        out_specs=[vmem, vmem],
        scratch_shapes=[pltpu.SemaphoreType.DMA((2 * PIECES,))],
        compiler_params=pltpu.CompilerParams(vmem_limit_bytes=PICK_BYTES),
        cost_estimate=NO_COST,
        name="pick_rest",
    )(*arrays, own_a)
    down = matched_caption_index.reshape(rows, 1)

    def kernel(body, name, *operands, shape=None, scratch=()):
        total_shape = jax.ShapeDtypeStruct((2 * rows, depth), jnp.float32)
        return pl.pallas_call(
            body,
            out_shape=shape or total_shape,
            in_specs=[SMEM, SMEM] + [vmem] * len(operands),
            out_specs=vmem,
            scratch_shapes=scratch,
            input_output_aliases={} if shape or body is own_kernel else {2: 0},
            compiler_params=params(),
            cost_estimate=NO_COST,
            name=name,
        )(flags, scale, *operands)

    one_a, one_b = hop(own_a, to_up), hop(own_b, to_up)
    group_a = hop(own_a, to_side_1)
    other_fixed = hop(fixed, core_swap)
    one_a, fixed_late = lax.optimization_barrier((one_a, fixed))
    two_a = hop(one_a, onward)
    over_a = hop(one_a, but_2_across)
    total = kernel(
        own_kernel,
        "own_blocks",
        down,
        matched_caption_index,
        fixed_late,
        own_a,
        own_b,
    )
    one_b, total = lax.optimization_barrier((one_b, total))
    two_b = hop(one_b, onward)
    over_b = hop(one_b, but_2_across)
    two_a, total = lax.optimization_barrier((two_a, total))
    last_a = hop(two_a, last_step)
    operands = (total, fixed, other_fixed, one_a, group_a, own_a, own_b)
    total = kernel(first_halves_kernel, "first_halves", *operands)
    total = kernel(halves_kernel, "second_halves", total, fixed, other_fixed, one_b, over_a)
    two_b, own_b, total = lax.optimization_barrier((two_b, own_b, total))
    last_b = hop(two_b, last_step)
    group_b = hop(own_b, to_side_1)
    total = kernel(halves_kernel, "third_halves", total, fixed, other_fixed, over_b, last_a)
    total = kernel(two_kernel, "two_block", total, fixed, other_fixed, two_a, two_b)
    width = [pltpu.VMEM((half, depth), jnp.float32)]

    def last_of(body, start, name, *operands):
        return kernel(
            functools.partial(body, start), name, total, *operands, shape=half_shape, scratch=width
        )

    sent, mine = [], []
    for k, name in enumerate(("last_other_a", "last_other_b")):
        sent.append(last_of(last_other_kernel, k * half, name, other_fixed, group_b, last_b))
    came = [hop(x, core_swap) for x in sent]
    for k, name in enumerate(("last_own_a", "last_own_b")):
        mine.append(last_of(last_own_kernel, k * half, name, fixed, group_b, last_b, came[k]))
    theirs = [hop(x, replica_swap) for x in mine]
    out_shape = jax.ShapeDtypeStruct((rows, depth), jnp.float32)

    def write(picture_step, start, values, outs, name):
        count = len(values)
        return pl.pallas_call(
            functools.partial(write_kernel, picture_step, start, count),
            out_shape=[out_shape, out_shape],
            in_specs=[vmem] * count + [ANY] * len(outs),
            out_specs=[ANY, ANY],
            scratch_shapes=[
                pltpu.VMEM((count * half, depth), jnp.float32),
                pltpu.SemaphoreType.DMA((count * PIECES,)),
            ],
            input_output_aliases={count + k: k for k in range(len(outs))},
            compiler_params=params(),
            cost_estimate=NO_COST,
            name=name,
        )(*values, *outs)

    outs = write(True, 0, mine, (), "write_mine")
    outs = write(False, 0, theirs[:1], outs, "write_theirs_a")
    return tuple(write(False, half, theirs[1:], outs, "write_theirs_b"))


def solution(mesh):
    placed = (P("dp", None), P("dp", None), P("dp", None), P(), P(), P())
    return jax.shard_map(
        per_device,
        mesh=mesh,
        in_specs=placed,
        out_specs=(P("dp", None), P("dp", None)),
        check_vma=False,
    )
```

```python
import functools

import jax
import jax.numpy as jnp
from jax import lax
from jax.experimental import pallas as pl
from jax.experimental.pallas import tpu as pltpu
from jax.sharding import PartitionSpec as P

GROUP = 4
VMEM_BYTES = 36 * 1024 * 1024
NO_ROOM = 60 * 1024 * 1024
PICK_BYTES = NO_ROOM

FIRST, CORE, SIDE = 0, 1, 2


def hop(x, pairs):
    return lax.ppermute(x, ("dp", "rep"), pairs)


def pairs_of(devices, target, members):
    pairs = []
    for p in range(devices):
        if p % GROUP in members:
            q = target(p)
            pairs.append((2 * p, 2 * q))
            pairs.append((2 * (devices - 1 - p) + 1, 2 * (devices - 1 - q) + 1))
    return pairs


def grads_of(scale_ref, left, block, match=None):
    product = lax.dot_general(
        left, block, (((1,), (1,)), ((), ())), preferred_element_type=jnp.float32
    )
    value = 1.0 / (scale_ref[2] + jnp.exp2(scale_ref[0] * product + scale_ref[1]))
    if match is not None:
        value = value - scale_ref[3] * match
    return value.astype(jnp.bfloat16)


def add_block(scale_ref, left_ref, refs, out_ref, match=None, fresh=False):
    block = jnp.concatenate([ref[...] for ref in refs], axis=0) if len(refs) > 1 else refs[0][...]
    grads = grads_of(scale_ref, left_ref[...], block, match)
    part = jnp.dot(grads, block, preferred_element_type=jnp.float32)
    out_ref[...] = part if fresh else out_ref[...] + part


PIECES = 4


def copy_all(pairs, sems):
    moves = []
    for source, target in pairs:
        size = source.shape[0] // PIECES
        for k in range(PIECES):
            part = pl.ds(k * size, size)
            moves.append(
                pltpu.make_async_copy(source.at[part], target.at[part], sems.at[len(moves)])
            )
    for move in moves:
        move.start()
    for move in moves:
        move.wait()


def pick_kernel(image_ref, text_ref, _, own_ref, own_b_ref, fixed_ref, sems):
    part = pl.ds(own_b_ref.shape[0], own_b_ref.shape[0])
    first = lax.axis_index("rep") == 0

    def copies(moving_ref, still_ref):
        pairs = [(moving_ref.at[part], own_b_ref), (moving_ref, own_ref), (still_ref, fixed_ref)]
        copy_all(pairs, sems)

    @pl.when(first)
    def _():
        copies(text_ref, image_ref)

    @pl.when(jnp.logical_not(first))
    def _():
        copies(image_ref, text_ref)


def write_kernel(picture_step, start, count, *refs):
    value_refs = refs[:count]
    picture_ref, caption_ref, wide_ref, sems = refs[-4:]
    to_picture = (lax.axis_index("rep") == 0) == picture_step
    size = value_refs[0].shape[0] // PIECES

    def write(target):
        moves = []
        for value_ref in value_refs:
            for k in range(PIECES):
                place = pl.ds(len(moves) * size, size)
                wide_ref[place] = value_ref[pl.ds(k * size, size)].astype(jnp.float32)
                there = target.at[pl.ds(start + len(moves) * size, size)]
                moves.append(
                    pltpu.make_async_copy(wide_ref.at[place], there, sems.at[len(moves)])
                )
                moves[-1].start()
        for move in moves:
            move.wait()

    @pl.when(to_picture)
    def _():
        write(picture_ref)

    @pl.when(jnp.logical_not(to_picture))
    def _():
        write(caption_ref)


def halves(total_ref):
    rows = total_ref.shape[0] // 2
    return total_ref.at[pl.ds(0, rows)], total_ref.at[pl.ds(rows, rows)]


def own_kernel(flag_ref, scale_ref, down_ref, along_ref, fixed_ref, own_ref, total_ref):
    mine, others = halves(total_ref)
    shape = (fixed_ref.shape[0], along_ref.shape[1])
    column = lax.broadcasted_iota(jnp.int32, shape, 1)
    row = lax.broadcasted_iota(jnp.int32, shape, 0)
    straight = (column == down_ref[...]).astype(jnp.float32)
    turned = (row == along_ref[...]).astype(jnp.float32)
    match = jnp.where(flag_ref[FIRST] == 1, straight, turned)
    add_block(scale_ref, fixed_ref, [own_ref], mine, match, fresh=True)
    others[...] = jnp.zeros_like(others)


def has(flag_ref, kind):
    core, side = flag_ref[CORE], flag_ref[SIDE]
    if kind == "own":
        return False, core == 0
    if kind == "group":
        return side == 1, side == 1
    if kind == "over":
        return core == 1, core == 1
    if kind == "two":
        return core + side == 0, jnp.logical_or(core == 1, side == 0)
    return True, True


def either(x, y):
    if x is True or y is True:
        return True
    return y if x is False else x if y is False else jnp.logical_or(x, y)


def blocks_kernel(jobs, flag_ref, scale_ref, _, fixed_ref, other_ref, *refs):
    total_ref, refs = refs[-1], list(refs[:-1])
    for kinds in jobs:
        now = [refs.pop(0) for _ in kinds]
        needed = (False, False)
        for kind in kinds:
            needed = tuple(either(x, y) for x, y in zip(needed, has(flag_ref, kind)))
        for rows_ref, sums_ref, wanted in zip((fixed_ref, other_ref), halves(total_ref), needed):
            if wanted is True:
                add_block(scale_ref, rows_ref, now, sums_ref)
            elif wanted is not False:
                pl.when(wanted)(
                    functools.partial(add_block, scale_ref, rows_ref, now, sums_ref)
                )


def last_sum(scale_ref, rows_ref, sum_ref, lasts, total_ref):
    block = lasts[0][...]
    for ref in lasts[1:]:
        block = block + ref[...]
    grads = grads_of(scale_ref, rows_ref[...], block)
    part = jnp.dot(grads, block, preferred_element_type=jnp.float32)
    total_ref[...] = sum_ref[...] + part


def last_other_kernel(flag_ref, scale_ref, rows_ref, sum_ref, *refs):
    *lasts, out_ref, total_ref = refs
    last_sum(scale_ref, rows_ref, sum_ref, lasts, total_ref)
    out_ref[...] = total_ref[...].astype(out_ref.dtype)


def last_own_kernel(flag_ref, scale_ref, rows_ref, sum_ref, *refs):
    *lasts, came_ref, out_ref, total_ref = refs
    last_sum(scale_ref, rows_ref, sum_ref, lasts, total_ref)
    whole_sum = total_ref[...] + came_ref[...].astype(jnp.float32)
    out_ref[...] = (scale_ref[4] * whole_sum).astype(out_ref.dtype)


def params():
    return pltpu.CompilerParams(vmem_limit_bytes=VMEM_BYTES)


NO_COST = pl.CostEstimate(flops=1, bytes_accessed=1, transcendentals=0)
SMEM = pl.BlockSpec(memory_space=pltpu.SMEM)
ANY = pl.BlockSpec(memory_space=pl.ANY)


def per_device(
    picture_vectors,
    caption_vectors,
    matched_caption_index,
    score_multiplier,
    score_offset,
    objective_cotangent,
):
    rows, depth = picture_vectors.shape
    devices = lax.axis_size("dp")
    first = lax.axis_index("rep") == 0
    place = lax.axis_index("dp")
    place = jnp.where(first, place, devices - 1 - place)
    flags = jnp.stack([first.astype(jnp.int32), place & 1, (place >> 1) & 1])
    log2e = 1.4426950408889634
    scale = jnp.stack(
        [
            -log2e * score_multiplier,
            -log2e * score_offset - jnp.log2(objective_cotangent),
            1.0 / objective_cotangent,
            objective_cotangent,
            score_multiplier,
        ]
    )

    def up(p):
        return (p + GROUP) % devices

    def across(p):
        return p ^ 2

    def swapped(p):
        return p ^ 1

    to_up = pairs_of(devices, up, (0, 1, 2, 3))
    passes_group = place % GROUP == 2
    to_side_1 = pairs_of(devices, across, (0, 1))
    core_1_across = pairs_of(devices, across, (1, 3))
    onward = pairs_of(devices, up, (1, 3)) + pairs_of(devices, across, (2,))
    last_step = pairs_of(devices, up, (0, 2)) + pairs_of(devices, across, (3,))
    core_swap = pairs_of(devices, swapped, (0, 1, 2, 3))
    replica_swap = [(2 * p + r, 2 * p + 1 - r) for p in range(devices) for r in range(2)]

    kind = picture_vectors.dtype
    half = rows // 2
    half_shape = jax.ShapeDtypeStruct((half, depth), kind)
    full_shape = jax.ShapeDtypeStruct((rows, depth), kind)
    vmem = pl.BlockSpec(memory_space=pltpu.VMEM)
    arrays = (picture_vectors, caption_vectors)
    own_a = jnp.where(first, caption_vectors[:half], picture_vectors[:half])
    own, own_b, fixed = pl.pallas_call(
        pick_kernel,
        out_shape=[full_shape, half_shape, full_shape],
        in_specs=[ANY, ANY, ANY],
        out_specs=[vmem, vmem, vmem],
        scratch_shapes=[pltpu.SemaphoreType.DMA((3 * PIECES,))],
        compiler_params=pltpu.CompilerParams(vmem_limit_bytes=PICK_BYTES),
        cost_estimate=NO_COST,
        name="pick",
    )(*arrays, own_a)
    down = matched_caption_index.reshape(rows, 1)

    def kernel(body, name, *operands, adds=True):
        return pl.pallas_call(
            body,
            out_shape=jax.ShapeDtypeStruct((2 * rows, depth), jnp.float32),
            in_specs=[SMEM, SMEM] + [vmem] * len(operands),
            out_specs=vmem,
            input_output_aliases={2: 0} if adds else {},
            compiler_params=params(),
            cost_estimate=NO_COST,
            name=name,
        )(flags, scale, *operands)

    def after(x, *others):
        return lax.optimization_barrier((x, *others))[0]

    def add_blocks(total, name, *jobs):
        blocks = [x for job in jobs for _, x in job]
        body = functools.partial(blocks_kernel, [[kind for kind, _ in job] for job in jobs])
        return kernel(body, name, total, fixed, other_fixed, *blocks)

    one_a, one_b = hop(own_a, to_up), hop(own_b, to_up)
    group = hop(own, to_side_1)
    other_fixed = hop(fixed, core_swap)
    sum_0 = kernel(
        own_kernel,
        "own_block",
        down,
        matched_caption_index,
        after(fixed, one_a),
        own,
        adds=False,
    )
    two_a = hop(one_a, onward)
    over_a = hop(one_a, core_1_across)
    two_b = hop(one_b, onward)
    over_b = hop(one_b, core_1_across)
    last_a = hop(jnp.where(passes_group, group[:half], after(two_a, one_b)), last_step)
    sum_1 = add_blocks(
        after(sum_0, two_a),
        "blocks_1",
        [("group", group)],
    )
    sum_2 = add_blocks(
        after(sum_1, over_a),
        "blocks_2",
        [("own", own)],
        [("one", one_a), ("one", one_b), ("over", over_a)],
    )
    last_b = hop(jnp.where(passes_group, after(group, two_b)[half:], after(two_b, sum_2)), last_step)
    sum_3 = add_blocks(
        after(sum_2, last_a),
        "blocks_3",
        [("over", over_b), ("last", last_a)],
    )
    sum_4 = add_blocks(
        sum_3,
        "blocks_4",
        [("two", two_a), ("two", two_b)],
    )
    total = sum_4

    def last_of(body, name, place, rows_of, *operands):
        block = (half, depth)
        return pl.pallas_call(
            body,
            grid=(1,),
            out_shape=half_shape,
            in_specs=[
                SMEM,
                SMEM,
                pl.BlockSpec(block, lambda i: (place % 2, 0)),
                pl.BlockSpec(block, lambda i: (place, 0)),
            ]
            + [pl.BlockSpec(block, lambda i: (0, 0))] * len(operands),
            out_specs=pl.BlockSpec(block, lambda i: (0, 0)),
            scratch_shapes=[pltpu.VMEM(block, jnp.float32)],
            compiler_params=params(),
            cost_estimate=NO_COST,
            name=name,
        )(flags, scale, rows_of, total, *operands)

    sent = [
        last_of(last_other_kernel, "last_other_a", 2, other_fixed, last_b),
        last_of(last_other_kernel, "last_other_b", 3, other_fixed, last_b),
    ]
    came = [hop(x, core_swap) for x in sent]
    mine = [
        last_of(last_own_kernel, "last_own_a", 0, fixed, last_b, came[0]),
        last_of(last_own_kernel, "last_own_b", 1, fixed, last_b, came[1]),
    ]
    theirs = [hop(x, replica_swap) for x in mine]
    out_shape = jax.ShapeDtypeStruct((rows, depth), jnp.float32)

    def write(picture_step, start, values, outs, name):
        count = len(values)
        return pl.pallas_call(
            functools.partial(write_kernel, picture_step, start, count),
            out_shape=[out_shape, out_shape],
            in_specs=[vmem] * count + [ANY] * len(outs),
            out_specs=[ANY, ANY],
            scratch_shapes=[
                pltpu.VMEM((count * half, depth), jnp.float32),
                pltpu.SemaphoreType.DMA((count * PIECES,)),
            ],
            input_output_aliases={count + k: k for k in range(len(outs))},
            compiler_params=params(),
            cost_estimate=NO_COST,
            name=name,
        )(*values, *outs)

    outs = write(True, 0, mine, (), "write_mine")
    outs = write(False, 0, theirs[:1], outs, "write_theirs_a")
    return tuple(write(False, half, theirs[1:], outs, "write_theirs_b"))


def solution(mesh):
    placed = (P("dp", None), P("dp", None), P("dp", None), P(), P(), P())
    return jax.shard_map(
        per_device,
        mesh=mesh,
        in_specs=placed,
        out_specs=(P("dp", None), P("dp", None)),
        check_vma=False,
    )
```

```python
import functools

import jax
import jax.numpy as jnp
from jax import lax
from jax.experimental import pallas as pl
from jax.experimental.pallas import tpu as pltpu
from jax.sharding import PartitionSpec as P

GROUP = 4
VMEM_BYTES = 36 * 1024 * 1024
NO_ROOM = 60 * 1024 * 1024
PICK_BYTES = 8 * 1024 * 1024

FIRST, CORE, SIDE = 0, 1, 2


def hop(x, pairs):
    return lax.ppermute(x, ("dp", "rep"), pairs)


def pairs_of(devices, target, members):
    pairs = []
    for p in range(devices):
        if p % GROUP in members:
            q = target(p)
            pairs.append((2 * p, 2 * q))
            pairs.append((2 * (devices - 1 - p) + 1, 2 * (devices - 1 - q) + 1))
    return pairs


def grads_of(scale_ref, left, block, match=None):
    product = lax.dot_general(
        left, block, (((1,), (1,)), ((), ())), preferred_element_type=jnp.float32
    )
    value = 1.0 / (scale_ref[2] + jnp.exp2(scale_ref[0] * product + scale_ref[1]))
    if match is not None:
        value = value - scale_ref[3] * match
    return value.astype(jnp.bfloat16)


def add_block(scale_ref, left_ref, refs, out_ref, match=None, fresh=False):
    block = jnp.concatenate([ref[...] for ref in refs], axis=0) if len(refs) > 1 else refs[0][...]
    grads = grads_of(scale_ref, left_ref[...], block, match)
    part = jnp.dot(grads, block, preferred_element_type=jnp.float32)
    out_ref[...] = part if fresh else out_ref[...] + part


PIECES = 4


def copy_all(pairs, sems):
    moves = []
    for source, target in pairs:
        size = source.shape[0] // PIECES
        for k in range(PIECES):
            part = pl.ds(k * size, size)
            moves.append(
                pltpu.make_async_copy(source.at[part], target.at[part], sems.at[len(moves)])
            )
    for move in moves:
        move.start()
    for move in moves:
        move.wait()


def pick_kernel(image_ref, text_ref, _, own_ref, own_b_ref, fixed_ref, sems):
    part = pl.ds(own_b_ref.shape[0], own_b_ref.shape[0])
    first = lax.axis_index("rep") == 0

    def copies(moving_ref, still_ref):
        pairs = [(moving_ref.at[part], own_b_ref), (moving_ref, own_ref), (still_ref, fixed_ref)]
        copy_all(pairs, sems)

    @pl.when(first)
    def _():
        copies(text_ref, image_ref)

    @pl.when(jnp.logical_not(first))
    def _():
        copies(image_ref, text_ref)


def write_kernel(picture_step, start, count, *refs):
    value_refs = refs[:count]
    picture_ref, caption_ref, wide_ref, sems = refs[-4:]
    to_picture = (lax.axis_index("rep") == 0) == picture_step
    size = value_refs[0].shape[0] // PIECES

    def write(target):
        moves = []
        for value_ref in value_refs:
            for k in range(PIECES):
                place = pl.ds(len(moves) * size, size)
                wide_ref[place] = value_ref[pl.ds(k * size, size)].astype(jnp.float32)
                there = target.at[pl.ds(start + len(moves) * size, size)]
                moves.append(
                    pltpu.make_async_copy(wide_ref.at[place], there, sems.at[len(moves)])
                )
                moves[-1].start()
        for move in moves:
            move.wait()

    @pl.when(to_picture)
    def _():
        write(picture_ref)

    @pl.when(jnp.logical_not(to_picture))
    def _():
        write(caption_ref)


def halves(total_ref):
    rows = total_ref.shape[0] // 2
    return total_ref.at[pl.ds(0, rows)], total_ref.at[pl.ds(rows, rows)]


def own_kernel(flag_ref, scale_ref, down_ref, along_ref, fixed_ref, own_ref, total_ref):
    mine, others = halves(total_ref)
    shape = (fixed_ref.shape[0], along_ref.shape[1])
    column = lax.broadcasted_iota(jnp.int32, shape, 1)
    row = lax.broadcasted_iota(jnp.int32, shape, 0)
    straight = (column == down_ref[...]).astype(jnp.float32)
    turned = (row == along_ref[...]).astype(jnp.float32)
    match = jnp.where(flag_ref[FIRST] == 1, straight, turned)
    add_block(scale_ref, fixed_ref, [own_ref], mine, match, fresh=True)
    others[...] = jnp.zeros_like(others)


def has(flag_ref, kind):
    core, side = flag_ref[CORE], flag_ref[SIDE]
    if kind == "own":
        return False, core == 0
    if kind == "group":
        return side == 1, side == 1
    if kind == "over":
        return core == 1, core == 1
    if kind == "two":
        return core + side == 0, jnp.logical_or(core == 1, side == 0)
    return True, True


def either(x, y):
    if x is True or y is True:
        return True
    return y if x is False else x if y is False else jnp.logical_or(x, y)


def blocks_kernel(jobs, flag_ref, scale_ref, _, fixed_ref, other_ref, *refs):
    total_ref, refs = refs[-1], list(refs[:-1])
    for kinds in jobs:
        now = [refs.pop(0) for _ in kinds]
        needed = (False, False)
        for kind in kinds:
            needed = tuple(either(x, y) for x, y in zip(needed, has(flag_ref, kind)))
        for rows_ref, sums_ref, wanted in zip((fixed_ref, other_ref), halves(total_ref), needed):
            if wanted is True:
                add_block(scale_ref, rows_ref, now, sums_ref)
            elif wanted is not False:
                pl.when(wanted)(
                    functools.partial(add_block, scale_ref, rows_ref, now, sums_ref)
                )


def last_sum(scale_ref, rows_ref, sum_ref, lasts, total_ref):
    block = lasts[0][...]
    for ref in lasts[1:]:
        block = block + ref[...]
    grads = grads_of(scale_ref, rows_ref[...], block)
    part = jnp.dot(grads, block, preferred_element_type=jnp.float32)
    total_ref[...] = sum_ref[...] + part


def last_other_kernel(flag_ref, scale_ref, rows_ref, sum_ref, *refs):
    *lasts, out_ref, total_ref = refs
    last_sum(scale_ref, rows_ref, sum_ref, lasts, total_ref)
    out_ref[...] = total_ref[...].astype(out_ref.dtype)


def last_own_kernel(flag_ref, scale_ref, rows_ref, sum_ref, *refs):
    *lasts, came_ref, out_ref, total_ref = refs
    last_sum(scale_ref, rows_ref, sum_ref, lasts, total_ref)
    whole_sum = total_ref[...] + came_ref[...].astype(jnp.float32)
    out_ref[...] = (scale_ref[4] * whole_sum).astype(out_ref.dtype)


def params():
    return pltpu.CompilerParams(vmem_limit_bytes=VMEM_BYTES)


NO_COST = pl.CostEstimate(flops=1, bytes_accessed=1, transcendentals=0)
SMEM = pl.BlockSpec(memory_space=pltpu.SMEM)
ANY = pl.BlockSpec(memory_space=pl.ANY)


def per_device(
    picture_vectors,
    caption_vectors,
    matched_caption_index,
    score_multiplier,
    score_offset,
    objective_cotangent,
):
    rows, depth = picture_vectors.shape
    devices = lax.axis_size("dp")
    first = lax.axis_index("rep") == 0
    place = lax.axis_index("dp")
    place = jnp.where(first, place, devices - 1 - place)
    flags = jnp.stack([first.astype(jnp.int32), place & 1, (place >> 1) & 1])
    log2e = 1.4426950408889634
    scale = jnp.stack(
        [
            -log2e * score_multiplier,
            -log2e * score_offset - jnp.log2(objective_cotangent),
            1.0 / objective_cotangent,
            objective_cotangent,
            score_multiplier,
        ]
    )

    def up(p):
        return (p + GROUP) % devices

    def across(p):
        return p ^ 2

    def swapped(p):
        return p ^ 1

    to_up = pairs_of(devices, up, (0, 1, 2, 3))
    passes_group = place % GROUP == 2
    to_side_1 = pairs_of(devices, across, (0, 1))
    core_1_across = pairs_of(devices, across, (1, 3))
    onward = pairs_of(devices, up, (1, 3)) + pairs_of(devices, across, (2,))
    last_step = pairs_of(devices, up, (0, 2)) + pairs_of(devices, across, (3,))
    core_swap = pairs_of(devices, swapped, (0, 1, 2, 3))
    replica_swap = [(2 * p + r, 2 * p + 1 - r) for p in range(devices) for r in range(2)]

    kind = picture_vectors.dtype
    half = rows // 2
    half_shape = jax.ShapeDtypeStruct((half, depth), kind)
    full_shape = jax.ShapeDtypeStruct((rows, depth), kind)
    vmem = pl.BlockSpec(memory_space=pltpu.VMEM)
    arrays = (picture_vectors, caption_vectors)
    own_a = jnp.where(first, caption_vectors[:half], picture_vectors[:half])
    own, own_b, fixed = pl.pallas_call(
        pick_kernel,
        out_shape=[full_shape, half_shape, full_shape],
        in_specs=[ANY, ANY, ANY],
        out_specs=[vmem, vmem, vmem],
        scratch_shapes=[pltpu.SemaphoreType.DMA((3 * PIECES,))],
        compiler_params=pltpu.CompilerParams(vmem_limit_bytes=PICK_BYTES),
        cost_estimate=NO_COST,
        name="pick",
    )(*arrays, own_a)
    down = matched_caption_index.reshape(rows, 1)

    def kernel(body, name, *operands, adds=True):
        return pl.pallas_call(
            body,
            out_shape=jax.ShapeDtypeStruct((2 * rows, depth), jnp.float32),
            in_specs=[SMEM, SMEM] + [vmem] * len(operands),
            out_specs=vmem,
            input_output_aliases={2: 0} if adds else {},
            compiler_params=params(),
            cost_estimate=NO_COST,
            name=name,
        )(flags, scale, *operands)

    def after(x, *others):
        return lax.optimization_barrier((x, *others))[0]

    def add_blocks(total, name, *jobs):
        blocks = [x for job in jobs for _, x in job]
        body = functools.partial(blocks_kernel, [[kind for kind, _ in job] for job in jobs])
        return kernel(body, name, total, fixed, other_fixed, *blocks)

    one_a, one_b = hop(own_a, to_up), hop(own_b, to_up)
    group = hop(own, to_side_1)
    other_fixed = hop(fixed, core_swap)
    sum_0 = kernel(
        own_kernel,
        "own_block",
        down,
        matched_caption_index,
        after(fixed, one_a),
        own,
        adds=False,
    )
    two_a = hop(one_a, onward)
    over_a = hop(one_a, core_1_across)
    two_b = hop(one_b, onward)
    over_b = hop(one_b, core_1_across)
    last_a = hop(jnp.where(passes_group, group[:half], after(two_a, one_b)), last_step)
    sum_1 = add_blocks(
        after(sum_0, two_a),
        "blocks_1",
        [("group", group)],
    )
    sum_2 = add_blocks(
        after(sum_1, over_a),
        "blocks_2",
        [("one", one_a), ("one", one_b), ("over", over_a)],
    )
    last_b = hop(jnp.where(passes_group, after(group, two_b)[half:], after(two_b, sum_2)), last_step)
    sum_3 = add_blocks(
        after(sum_2, last_a),
        "blocks_3",
        [("own", own)],
        [("over", over_b), ("last", last_a)],
    )
    sum_4 = add_blocks(
        sum_3,
        "blocks_4",
        [("two", two_a), ("two", two_b)],
    )
    total = sum_4

    def last_of(body, name, place, rows_of, *operands):
        block = (half, depth)
        return pl.pallas_call(
            body,
            grid=(1,),
            out_shape=half_shape,
            in_specs=[
                SMEM,
                SMEM,
                pl.BlockSpec(block, lambda i: (place % 2, 0)),
                pl.BlockSpec(block, lambda i: (place, 0)),
            ]
            + [pl.BlockSpec(block, lambda i: (0, 0))] * len(operands),
            out_specs=pl.BlockSpec(block, lambda i: (0, 0)),
            scratch_shapes=[pltpu.VMEM(block, jnp.float32)],
            compiler_params=params(),
            cost_estimate=NO_COST,
            name=name,
        )(flags, scale, rows_of, total, *operands)

    sent = [
        last_of(last_other_kernel, "last_other_a", 2, other_fixed, last_b),
        last_of(last_other_kernel, "last_other_b", 3, other_fixed, last_b),
    ]
    came = [hop(x, core_swap) for x in sent]
    mine = [
        last_of(last_own_kernel, "last_own_a", 0, fixed, last_b, came[0]),
        last_of(last_own_kernel, "last_own_b", 1, fixed, last_b, came[1]),
    ]
    theirs = [hop(x, replica_swap) for x in mine]
    out_shape = jax.ShapeDtypeStruct((rows, depth), jnp.float32)

    def write(picture_step, start, values, outs, name):
        count = len(values)
        return pl.pallas_call(
            functools.partial(write_kernel, picture_step, start, count),
            out_shape=[out_shape, out_shape],
            in_specs=[vmem] * count + [ANY] * len(outs),
            out_specs=[ANY, ANY],
            scratch_shapes=[
                pltpu.VMEM((count * half, depth), jnp.float32),
                pltpu.SemaphoreType.DMA((count * PIECES,)),
            ],
            input_output_aliases={count + k: k for k in range(len(outs))},
            compiler_params=params(),
            cost_estimate=NO_COST,
            name=name,
        )(*values, *outs)

    outs = write(True, 0, mine, (), "write_mine")
    outs = write(False, 0, theirs[:1], outs, "write_theirs_a")
    return tuple(write(False, half, theirs[1:], outs, "write_theirs_b"))


def solution(mesh):
    placed = (P("dp", None), P("dp", None), P("dp", None), P(), P(), P())
    return jax.shard_map(
        per_device,
        mesh=mesh,
        in_specs=placed,
        out_specs=(P("dp", None), P("dp", None)),
        check_vma=False,
    )
```
